256 devices in a mesh: tm: 8 (over y, x_lo), cam: 16 (over z, core), head: 2 (over x_hi).
Axes of the slice: x: 4 (x_hi: 2, x_lo: 2; x = x_hi * 2 + x_lo), y: 4, z: 8, core: 2. Of those that a mesh axis runs over, the one named last changes fastest.
Arguments:
- tokens: bfloat16 [16, 128, 32, 2048], P('tm', 'cam'), may hold values from -40 to 40
- w_qkv: bfloat16 [2048, 3, 1024], P(None, None, 'head'), may hold values from -0.25 to 0.25
- w_out: bfloat16 [1024, 2048], P('head'), may hold values from -0.1875 to 0.1875
- window_len: int32 [8], P('head'), may hold values from 1 to 4, as said below
- edge_counts: int32 [16], replicated, may hold values from 1 to 8, as said below
- context_kv: bfloat16 [3, 128, 32, 2, 1024], P(None, 'cam', None, None, 'head'), may hold values from -6 to 6
Outputs:
- mixed: bfloat16 [16, 128, 32, 2048], P('tm', 'cam', None, 'head')
The draws below stay inside these ranges and needn't reach their ends.
Inputs may be any that keep to these rules, and one draw needn't show every extreme that they name: `window_len`: some head has 4 frames and some head 1 frame. `edge_counts`: some boundary shares 8 columns and some 1 column.
All inputs are finite; a program needn't handle non-finite values.
Results may differ from the reference program's by a relative error of at most 0.008.
Values may be sent and summed in bfloat16 or wider, within the bound.
No kernel may reach another device: no remote copies, remote signals or barrier semaphores. Data moves between devices by JAX's collectives and lax.ppermute only.
A program may use at most 128 MiB of HBM per device.

```python
import jax
import jax.numpy as jnp
from jax import lax

D = 2048
HEADS = 8
HD = 128
COLS_DEV = 8
ROWS = 32
WMAX = 4
EDGE = 8
FRAMES = 16
COLS_ALL = 128
CTILES = 16
N_CAM = 16
N_HEAD = 2


def draw_tokens(key, part):
    key = jax.random.fold_in(key, 11)
    first = jax.random.fold_in(key, 0)
    values = jax.random.normal(first, (FRAMES, COLS_ALL, ROWS, D), jnp.float32)
    return jnp.clip(values, -40.0, 40.0).astype(jnp.bfloat16)


def draw_w_qkv(key, part):
    key = jax.random.fold_in(key, 12)
    first, second, third = jax.random.split(key, 3)
    query_part = jax.random.normal(first, (D, 1, HEADS * HD), jnp.float32)
    other_part = jax.random.normal(second, (D, 1, HEADS * HD), jnp.float32)
    value_part = jax.random.normal(third, (D, 1, HEADS * HD), jnp.float32)
    key_part = other_part
    values = jnp.concatenate([query_part, key_part, value_part], axis=1) / D ** 0.5
    return jnp.clip(values, -0.25, 0.25).astype(jnp.bfloat16)


def forced_counts(key, count, most):
    first, second, third = jax.random.split(key, 3)
    values = jax.random.randint(first, (count,), 1, most + 1)
    high_pick = jax.random.randint(second, (), 0, count)
    low_pick = (high_pick + 1 + jax.random.randint(third, (), 0, count - 1)) % count
    places = jnp.arange(count)
    values = jnp.where(places == high_pick, most, values)
    values = jnp.where(places == low_pick, 1, values)
    return values.astype(jnp.int32)


def draw_window_len(key, part):
    key = jax.random.fold_in(key, 13)
    return forced_counts(key, HEADS, WMAX)


def draw_edge_counts(key, part):
    key = jax.random.fold_in(key, 14)
    return forced_counts(key, CTILES, EDGE)


def steps_of(key, shape, pieces, least, largest):
    level = 1.0
    for axis_at, shards_of in pieces:
        steps = jax.random.uniform(jax.random.fold_in(jax.random.fold_in(key, 6), axis_at), (shards_of,), jnp.float32, least / len(pieces), largest / len(pieces))
        level = level * jnp.repeat(jnp.exp(steps), shape[axis_at] // shards_of).reshape((-1,) + (1,) * (len(shape) - 1 - axis_at))
    return level


def noise(rng, extent, scale, most, pieces=(), kind=jnp.bfloat16):
    loudness = steps_of(rng, extent, pieces, -0.22, 0.18) if pieces else 1.0
    drawn = jax.random.normal(rng, extent, jnp.float32) * scale * loudness
    return jnp.minimum(jnp.maximum(drawn, -most), most).astype(kind)


def setup_inputs(seed: int = 0) -> dict:
    key_of = jax.random.split(jax.random.key(seed), 7)
    return {
        "tokens": draw_tokens(jax.random.fold_in(key_of[6], 71), 0),
        "w_qkv": draw_w_qkv(jax.random.fold_in(key_of[6], 71), 0),
        "w_out": noise(key_of[2], (HEADS * HD, D), (HEADS * HD) ** -0.5, 0.1875, ((0, 2),)),
        "window_len": draw_window_len(jax.random.fold_in(key_of[6], 71), 0),
        "edge_counts": draw_edge_counts(jax.random.fold_in(key_of[6], 71), 0),
        "context_kv": noise(key_of[5], (WMAX - 1, COLS_ALL, ROWS, 2, HEADS * HD), 1.0, 6.0, ((1, 16), (4, 2))),
    }


def reference(tokens, w_qkv, w_out, window_len, edge_counts, context_kv):
    frame_count, col_total, row_count, width = tokens.shape
    span_cols = COLS_DEV + 2 * EDGE
    scale = 1.0 / (HD ** 0.5)

    def project(frame_rows):
        flat_rows = frame_rows.reshape(col_total * row_count, width)
        result = jnp.dot(flat_rows, w_qkv.reshape(width, 3 * HEADS * HD), preferred_element_type=jnp.float32)
        return result.astype(jnp.bfloat16).reshape(col_total, row_count, 3, HEADS, HD)

    projected = lax.map(project, tokens)
    history = context_kv.reshape(WMAX - 1, col_total, row_count, 2, HEADS, HD)
    history = jnp.concatenate([jnp.zeros((WMAX - 1, col_total, row_count, 1, HEADS, HD), jnp.bfloat16), history], axis=3)
    padded = jnp.concatenate([history, projected], axis=0)
    offsets = jnp.arange(span_cols, dtype=jnp.int32) - EDGE
    key_offsets = jnp.tile(jnp.repeat(offsets, row_count), WMAX)
    key_slots = jnp.repeat(jnp.arange(WMAX, dtype=jnp.int32), span_cols * row_count)

    def attend(item_index):
        frame_index = item_index // N_CAM
        tile_index = item_index % N_CAM
        current = lax.dynamic_index_in_dim(projected, frame_index, 0, keepdims=False)
        queries = lax.dynamic_slice_in_dim(current, (tile_index * COLS_DEV).astype(jnp.int32), COLS_DEV, 0)[:, :, 0]
        queries = queries.reshape(COLS_DEV * row_count, HEADS, HD)
        window = lax.dynamic_slice_in_dim(padded, frame_index.astype(jnp.int32), WMAX, 0)
        col_index = ((tile_index * COLS_DEV + offsets) % col_total).astype(jnp.int32)
        widened = jnp.take(window, col_index, axis=1)
        keys = widened[:, :, :, 1].reshape(-1, HEADS, HD)
        values = widened[:, :, :, 2].reshape(-1, HEADS, HD)
        right_count = edge_counts[tile_index]
        left_count = edge_counts[(tile_index + N_CAM - 1) % N_CAM]
        col_ok = ((key_offsets >= 0) & (key_offsets < COLS_DEV)) | ((key_offsets < 0) & (key_offsets >= -left_count)) | ((key_offsets >= COLS_DEV) & (key_offsets < COLS_DEV + right_count))
        key_frame = frame_index - (WMAX - 1) + key_slots
        allowed = col_ok[None, :] & (key_frame[None, :] > frame_index - window_len[:, None])
        scores = jnp.einsum("qhd,khd->hqk", queries.astype(jnp.float32), keys.astype(jnp.float32)) * scale
        scores = jnp.where(allowed[:, None, :], scores, -jnp.inf)
        peak = jnp.max(scores, axis=2, keepdims=True)
        weights = jnp.exp(scores - peak)
        probs = (weights / jnp.sum(weights, axis=2, keepdims=True)).astype(jnp.bfloat16)
        attended = jnp.einsum("hqk,khd->qhd", probs.astype(jnp.float32), values.astype(jnp.float32))
        return attended.astype(jnp.bfloat16).reshape(COLS_DEV * row_count, HEADS * HD)

    attended = lax.map(attend, jnp.arange(frame_count * N_CAM, dtype=jnp.int32))
    attended = attended.reshape(frame_count, col_total, row_count, HEADS * HD)
    group_width = HEADS * HD // N_HEAD

    def output(frame_rows):
        flat_rows = frame_rows.reshape(col_total * row_count, HEADS * HD)
        total = jnp.zeros((col_total * row_count, width), jnp.float32)
        for group in range(N_HEAD):
            part = jnp.dot(flat_rows[:, group * group_width:(group + 1) * group_width], w_out[group * group_width:(group + 1) * group_width], preferred_element_type=jnp.float32)
            total = total + lax.optimization_barrier(part.astype(jnp.bfloat16)).astype(jnp.float32)
        return total.astype(jnp.bfloat16).reshape(col_total, row_count, width)

    return lax.map(output, attended)
```

```python
import functools

import jax
import jax.numpy as jnp
from jax import lax
from jax.experimental import pallas as pl
from jax.experimental.pallas import tpu as pltpu
from jax.sharding import PartitionSpec as P

AXES = ("tm", "cam", "head")
HD = 128
WMAX = 4
TILE = 256
LOG2E = 1.4426950408889634
MIB = 1 << 20


def pairs_of(sizes, move):
    tm, cam, head = sizes
    flat = lambda t, c, h: (t * cam + c) * head + h
    return [
        (flat(t, c, h), flat(*move(t, c, h)))
        for t in range(tm)
        for c in range(cam)
        for h in range(head)
    ]


def project_kernel(info, tokens, w, first, second):
    made = jnp.dot(tokens[...], w[0], preferred_element_type=jnp.float32)
    made = made.astype(jnp.bfloat16)
    first[...] = made[:, :HD].reshape(first.shape)
    second[...] = made[:, HD:].reshape(second.shape)


def project_kv(info, tokens, w3, other):
    rows, width = tokens.shape
    frames = rows // TILE
    shape = jax.ShapeDtypeStruct((2, frames, TILE, HD), jnp.bfloat16)

    def pick(j, info):
        return (j + 1, 0, 1 - info[0] if other else info[0])

    return pl.pallas_call(
        project_kernel,
        out_shape=(shape, shape),
        grid_spec=pltpu.PrefetchScalarGridSpec(
            num_scalar_prefetch=1,
            grid=(2,),
            in_specs=[
                pl.BlockSpec((rows, width), lambda j, info: (0, 0)),
                pl.BlockSpec((1, width, 2 * HD), pick),
            ],
            out_specs=[pl.BlockSpec((1, frames, TILE, HD), lambda j, info: (j, 0, 0, 0))] * 2,
        ),
        compiler_params=pltpu.CompilerParams(vmem_limit_bytes=32 * MIB),
        cost_estimate=pl.CostEstimate(
            flops=2 * rows * width * 4 * HD, bytes_accessed=5 * MIB, transcendentals=0
        ),
    )(info, tokens, w3)


def query_kernel(info, tokens, w, out):
    made = jnp.dot(tokens[...], w[0], preferred_element_type=jnp.float32)
    out[...] = made.astype(jnp.bfloat16).reshape(out.shape)


def project_q(info, tokens, w3):
    rows, width = tokens.shape
    frames = rows // TILE
    return pl.pallas_call(
        query_kernel,
        out_shape=jax.ShapeDtypeStruct((2, frames, TILE, 2 * HD), jnp.bfloat16),
        grid_spec=pltpu.PrefetchScalarGridSpec(
            num_scalar_prefetch=1,
            grid=(2,),
            in_specs=[
                pl.BlockSpec((rows, width), lambda j, info: (0, 0)),
                pl.BlockSpec((1, width, 2 * HD), lambda j, info: (0, 0, (1 - info[0] + j) % 2)),
            ],
            out_specs=pl.BlockSpec((1, frames, TILE, 2 * HD), lambda j, info: (j, 0, 0, 0)),
        ),
        compiler_params=pltpu.CompilerParams(vmem_limit_bytes=32 * MIB),
        cost_estimate=pl.CostEstimate(
            flops=2 * rows * width * 4 * HD, bytes_accessed=5 * MIB, transcendentals=0
        ),
    )(info, tokens, w3)


def halo_kernel(info, kvx, kvm, ctx, out, sems):
    x_lo, last = info[0], info[1]

    def copy(pieces):
        made = [
            pltpu.make_async_copy(src, out.at[i], sems.at[i]) for i, src in enumerate(pieces)
        ]
        for one in made:
            one.start()
        for one in made:
            one.wait()

    @pl.when(last == 1)
    def _():
        copy((ctx.at[:, 2 - 2 * x_lo], ctx.at[:, 1]))

    @pl.when((last == 0) & (x_lo == 0))
    def _():
        copy((kvx.at[:, 1], kvx.at[:, 0]))

    @pl.when((last == 0) & (x_lo == 1))
    def _():
        copy((kvx.at[:, 1], kvm.at[:, 0]))


def halo_pieces(info, kvx, kvm, ctx):
    any_spec = pl.BlockSpec(memory_space=pl.ANY)
    return pl.pallas_call(
        halo_kernel,
        out_shape=jax.ShapeDtypeStruct((2, 2, TILE, HD), jnp.bfloat16),
        in_specs=[pl.BlockSpec(memory_space=pltpu.SMEM), any_spec, any_spec, any_spec],
        out_specs=any_spec,
        scratch_shapes=[pltpu.SemaphoreType.DMA((2,))],
        cost_estimate=pl.CostEstimate(flops=0, bytes_accessed=MIB // 2, transcendentals=0),
    )(info, kvx, kvm, ctx)


def attend_kernel(head, info, q_own, q_far, *refs):
    own, far, near, rest = refs[0:3], refs[3:6], refs[6:9], refs[9:12]
    out_own, out_far, kv, sems = refs[12:]
    x_lo, left, right, window = info[0], info[2], info[3], info[4 + head]
    copies = []
    for place in range(3):
        cols = pl.ds((1, 0, 2)[place] * TILE, TILE)
        copies += [
            (own[place], kv.at[:, pl.ds(3 + 2 * x_lo, 2), cols]),
            (far[place], kv.at[:, pl.ds(5 - 2 * x_lo, 2), cols]),
            (near[place], kv.at[:, 2 * x_lo, cols]),
            (rest[place].at[0], kv.at[:, 2 - 2 * x_lo, cols]),
            (rest[place].at[1], kv.at[:, 1, cols]),
        ]
    copies = [
        pltpu.make_async_copy(src, dst, sems.at[i]) for i, (src, dst) in enumerate(copies)
    ]
    for copy in copies:
        copy.start()
    for copy in copies:
        copy.wait()
    scale = LOG2E / HD**0.5
    spot = lax.broadcasted_iota(jnp.int32, (1, 3 * TILE), 1)
    rows_col = TILE // 8
    seen = (spot >= TILE - left * rows_col) & (spot < 2 * TILE + right * rows_col)
    bias = jnp.where(seen, 0.0, -jnp.inf).astype(jnp.float32)
    for part in range(4):
        frame = (2 * x_lo if part < 2 else 2 - 2 * x_lo) + part % 2
        q = (q_own if part < 2 else q_far)[part % 2, :, :]

        def step(back, carry):
            peak, total, acc = carry
            at = 3 + frame - back
            scores = lax.dot_general(
                q, kv[0, at], (((1,), (1,)), ((), ())), preferred_element_type=jnp.float32
            )
            scores = scores * scale + bias
            new = jnp.maximum(peak, jnp.max(scores, axis=1, keepdims=True))
            weights = jnp.exp2(scores - new)
            shrink = jnp.exp2(peak - new)
            total = total * shrink + jnp.sum(weights, axis=1, keepdims=True)
            acc = acc * shrink + jnp.dot(
                weights.astype(jnp.bfloat16), kv[1, at], preferred_element_type=jnp.float32
            )
            return new, total, acc

        start = (
            jnp.full((TILE, 1), -jnp.inf, jnp.float32),
            jnp.zeros((TILE, 1), jnp.float32),
            jnp.zeros((TILE, HD), jnp.float32),
        )
        _, total, acc = lax.fori_loop(0, window, step, start)
        done = (acc / total).astype(jnp.bfloat16)
        (out_own if part < 2 else out_far)[part % 2, :, :] = done


def attend(head, info, q_own, q_far, pieces):
    any_spec = pl.BlockSpec(memory_space=pl.ANY)
    q_spec = pl.BlockSpec((2, TILE, HD), lambda i: (0, 0, head))
    shape = jax.ShapeDtypeStruct((2, TILE, HD), jnp.bfloat16)
    out_spec = pl.BlockSpec((2, TILE, HD), lambda i: (0, 0, 0))
    return pl.pallas_call(
        functools.partial(attend_kernel, head),
        out_shape=(shape, shape),
        grid=(1,),
        in_specs=[pl.BlockSpec(memory_space=pltpu.SMEM), q_spec, q_spec]
        + [any_spec] * len(pieces),
        out_specs=(out_spec, out_spec),
        scratch_shapes=[
            pltpu.VMEM((2, 3 + 4, 3 * TILE, HD), jnp.bfloat16),
            pltpu.SemaphoreType.DMA((15,)),
        ],
        compiler_params=pltpu.CompilerParams(vmem_limit_bytes=32 * MIB),
        cost_estimate=pl.CostEstimate(
            flops=4 * 4 * TILE * 4 * 3 * TILE * HD,
            bytes_accessed=4 * MIB,
            transcendentals=4 * TILE * 4 * 3 * TILE,
        ),
    )(info, q_own, q_far, *pieces)


def mix_kernel(info, own0, own1, mate0, mate1, over0, over1, diag0, diag1, w_own, w_mine, w_core, out, w_far, sems):
    x_lo, core = info[0], info[6]
    copies = [
        pltpu.make_async_copy(w_mine, w_far.at[core], sems.at[0]),
        pltpu.make_async_copy(w_core, w_far.at[1 - core], sems.at[1]),
    ]

    @pl.when(pl.program_id(0) == 0)
    def _():
        for copy in copies:
            copy.start()
        for copy in copies:
            copy.wait()

    cols = pl.ds(pl.multiple_of(pl.program_id(0) * out.shape[1], out.shape[1]), out.shape[1])
    near = pl.ds(pl.multiple_of(2 * HD * x_lo, 2 * HD), 2 * HD)
    far = pl.ds(pl.multiple_of(2 * HD * (1 - x_lo), 2 * HD), 2 * HD)

    def times(first, second, w):
        both = jnp.concatenate([first[...], second[...]], axis=1)
        return jnp.dot(both, w, preferred_element_type=jnp.float32)

    group = times(own0, own1, w_own[near, :]) + times(mate0, mate1, w_own[far, :])
    other = times(over0, over1, w_far[x_lo, :, cols]) + times(diag0, diag1, w_far[1 - x_lo, :, cols])
    group = group.astype(jnp.bfloat16).astype(jnp.float32)
    other = other.astype(jnp.bfloat16).astype(jnp.float32)
    out[...] = (group + other).astype(jnp.bfloat16)


def mix(info, attended, w_out, w_mine, w_core):
    rows = attended[0].shape[0]
    width = w_out.shape[1] // 2
    steps = 4
    step = width // steps
    whole = pl.BlockSpec((rows, HD), lambda j, info: (0, 0))
    any_spec = pl.BlockSpec(memory_space=pl.ANY)
    return pl.pallas_call(
        mix_kernel,
        out_shape=jax.ShapeDtypeStruct((rows, width), jnp.bfloat16),
        grid_spec=pltpu.PrefetchScalarGridSpec(
            num_scalar_prefetch=1,
            grid=(steps,),
            in_specs=[whole] * 8
            + [
                pl.BlockSpec((w_out.shape[0], step), lambda j, info: (0, info[7] * steps + j)),
                any_spec,
                any_spec,
            ],
            out_specs=pl.BlockSpec((rows, step), lambda j, info: (0, j)),
            scratch_shapes=[
                pltpu.VMEM((2,) + w_mine.shape, jnp.bfloat16),
                pltpu.SemaphoreType.DMA((2,)),
            ],
        ),
        compiler_params=pltpu.CompilerParams(vmem_limit_bytes=32 * MIB),
        cost_estimate=pl.CostEstimate(
            flops=2 * rows * width * 8 * HD, bytes_accessed=5 * MIB, transcendentals=0
        ),
    )(info, *attended, w_out, w_mine, w_core)


def body(tokens, w_qkv, w_out, window_len, edge_counts, context_kv):
    frames, cols, row_count, width = tokens.shape
    sizes = tuple(lax.axis_size(axis) for axis in AXES)
    tm_count, cam_count, _ = sizes
    tm, cam, x_hi = (lax.axis_index(axis) for axis in AXES)
    x_lo, core = tm % 2, cam % 2
    last = (tm >= tm_count - 2).astype(jnp.int32)

    def moved(move):
        pairs = pairs_of(sizes, move)
        return lambda shard: lax.ppermute(shard, AXES, pairs)

    to_mate = moved(lambda t, c, h: (t ^ 1, c, h))
    to_over = moved(lambda t, c, h: (t, c, 1 - h))
    to_diag = moved(lambda t, c, h: (t ^ 1, c, 1 - h))
    to_later = moved(lambda t, c, h: ((t + 2) % tm_count, c, h))
    to_right = moved(lambda t, c, h: (t, (c + 1) % cam_count, h))
    to_left = moved(lambda t, c, h: (t, (c - 1) % cam_count, h))
    to_core = moved(lambda t, c, h: (t, c ^ 1, h))
    both = lambda shard: (to_right(shard), to_left(shard))

    windows = lax.dynamic_slice_in_dim(window_len, 2 * x_lo, 2)
    info = jnp.stack(
        [
            x_lo,
            last,
            edge_counts[(cam + cam_count - 1) % cam_count],
            edge_counts[cam],
            windows[0],
            windows[1],
            core,
            x_hi,
        ]
    ).astype(jnp.int32)

    flat = tokens.reshape(frames * cols * row_count, width)
    w3 = jnp.transpose(w_qkv, (1, 0, 2))

    sent = project_kv(info, flat, w3, True)
    kvx = [to_mate(one) for one in sent]
    kvm = project_kv(info, flat, w3, False)
    queries = project_q(info, flat, w3)
    q_far = to_mate(queries[0])
    q_own = queries[1]

    w_part = lax.dynamic_slice(w_out, (core * 2 * HD, (1 - x_hi) * (w_out.shape[1] // 2)), (2 * HD, w_out.shape[1] // 2))
    w_mine = to_diag(w_part)
    w_core = to_core(w_mine)

    z_own = [both(one) for one in kvm]

    history = lax.dynamic_slice_in_dim(context_kv, 2 * HD * x_lo, 2 * HD, 4)
    history = history.reshape(WMAX - 1, TILE, 2, 2, HD)
    history = jnp.transpose(history, (3, 2, 0, 1, 4))

    outs = []
    for head in range(2):
        ctx = history[head]
        oldest = lax.dynamic_index_in_dim(ctx, 2 * x_lo, 1, keepdims=False)
        near = to_later(jnp.where(last == 1, oldest, kvm[head][:, 1]))
        z_near = both(near)
        z_far = both(kvx[head])
        rest = to_later(halo_pieces(info, kvx[head], kvm[head], ctx))
        z_rest = both(rest)
        pieces = (
            [kvm[head], *z_own[head]]
            + [kvx[head], *z_far]
            + [near, *z_near]
            + [rest, *z_rest]
        )
        outs.append(attend(head, info, q_own, q_far, pieces))

    attended = []
    for group in (
        [one[0] for one in outs],
        [to_mate(one[1]) for one in outs],
        [to_over(one[0]) for one in outs],
        [to_diag(one[1]) for one in outs],
    ):
        attended += [one.reshape(-1, HD) for one in group]
    out = mix(info, attended, w_out, w_mine, w_core)
    return out.reshape(frames, cols, row_count, -1)


def solution(mesh):
    placed = (
        P("tm", "cam", None, None),
        P(None, None, "head"),
        P("head", None),
        P("head"),
        P(),
        P(None, "cam", None, None, "head"),
    )
    return jax.shard_map(
        body, mesh=mesh, in_specs=placed, out_specs=P("tm", "cam", None, "head"), check_vma=False
    )
```

```python
import functools

import jax
import jax.numpy as jnp
from jax import lax
from jax.experimental import pallas as pl
from jax.experimental.pallas import tpu as pltpu
from jax.sharding import PartitionSpec as P

AXES = ("tm", "cam", "head")
HD = 128
WMAX = 4
PAIR = 2
TILE = 256
LOG2E = 1.4426950408889634
MIB = 1 << 20
ANY = pl.BlockSpec(memory_space=pl.ANY)
VMEM = pl.BlockSpec(memory_space=pltpu.VMEM)
SMEM = pl.BlockSpec(memory_space=pltpu.SMEM)
PARAMS = pltpu.CompilerParams(vmem_limit_bytes=64 * MIB)
SMALL = pl.CostEstimate(flops=1000, bytes_accessed=1000, transcendentals=0)


def cost(us):
    return pl.CostEstimate(flops=int(us * 1.15e9), bytes_accessed=1000, transcendentals=0)


C_SEND, C_OWN, C_GATHER, C_ATTEND, C_MIX = 1, 1, 2, 1, 1
SPLIT, CTX_FIRST, Q_AFTER, OUTER_B, W_AFTER, EXCH = 0, 1, 2, 1, 1, 0


def pairs_of(sizes, move):
    tm, cam, head = sizes
    flat = lambda t, c, h: (t * cam + c) * head + h
    return [
        (flat(t, c, h), flat(*move(t, c, h)))
        for t in range(tm)
        for c in range(cam)
        for h in range(head)
    ]


def x_low():
    return lax.axis_index("tm") % 2


def bf16(*shape):
    return jax.ShapeDtypeStruct(shape, jnp.bfloat16)


def project_kernel(blocks, chunks, tokens, w3, *refs):
    outs, (flat, w, sem_t, sem_w) = refs[:-4], refs[-4:]
    mine = x_low()
    depth = flat.shape[1] // chunks
    steps = []
    for k in range(chunks):
        ks = pl.ds(k * depth, depth)
        copies = [pltpu.make_async_copy(tokens.at[:, ks], flat.at[:, ks], sem_t.at[k])]
        for i, (which, own, _, _) in enumerate(blocks):
            col = pl.multiple_of(PAIR * HD * (mine if own else 1 - mine), PAIR * HD)
            copies.append(
                pltpu.make_async_copy(
                    w3.at[which, ks, pl.ds(col, PAIR * HD)],
                    w.at[ks, pl.ds(i * PAIR * HD, PAIR * HD)],
                    sem_w.at[k, i],
                )
            )
        steps.append(copies)
        for copy in copies:
            copy.start()
    total = None
    for k, copies in enumerate(steps):
        for copy in copies:
            copy.wait()
        ks = slice(k * depth, (k + 1) * depth)
        made = jnp.dot(flat[:, ks], w[ks, :], preferred_element_type=jnp.float32)
        total = made if total is None else total + made
    total = total.astype(jnp.bfloat16)
    for i, (_, _, out, at) in enumerate(blocks):
        for head in range(PAIR):
            col = (i * PAIR + head) * HD
            piece = total[:, col : col + HD].reshape(-1, TILE, HD)
            if at:
                outs[out + head][(0,) + at] = piece
            else:
                outs[out][head] = piece


def project(blocks, shapes, tokens, w3, estimate):
    rows, width = tokens.shape
    chunks = 4
    return pl.pallas_call(
        functools.partial(project_kernel, blocks, chunks),
        out_shape=shapes,
        in_specs=[ANY, ANY],
        out_specs=[VMEM] * len(shapes),
        scratch_shapes=[
            pltpu.VMEM((rows, width), jnp.bfloat16),
            pltpu.VMEM((width, len(blocks) * PAIR * HD), jnp.bfloat16),
            pltpu.SemaphoreType.DMA((chunks,)),
            pltpu.SemaphoreType.DMA((chunks, len(blocks))),
        ],
        compiler_params=PARAMS,
        cost_estimate=estimate,
    )(tokens, w3)


def run_copies(pairs, sems):
    copies = [pltpu.make_async_copy(src, dst, sems.at[i]) for i, (src, dst) in enumerate(pairs)]
    for copy in copies:
        copy.start()
    for copy in copies:
        copy.wait()


def gather_kernel(kvx, kvm, ctx, four, halo, sems):
    tm, count = lax.axis_index("tm"), lax.axis_size("tm")
    mine = tm % 2
    pairs = [(kvm, four.at[:, pl.ds(2 * mine, 2)]), (kvx, four.at[:, pl.ds(2 - 2 * mine, 2)])]

    @pl.when(tm >= count - 2)
    def _():
        run_copies(pairs + [(ctx, halo)], sems)

    @pl.when((tm < count - 2) & (mine == 0))
    def _():
        run_copies(pairs + [(kvm.at[:, 1], halo.at[:, 0]), (kvx, halo.at[:, pl.ds(1, 2)])], sems)

    @pl.when((tm < count - 2) & (mine == 1))
    def _():
        run_copies(pairs + [(kvx.at[:, 1], halo.at[:, 0]), (kvm, halo.at[:, pl.ds(1, 2)])], sems)


def gather(kvx, kvm, ctx):
    return pl.pallas_call(
        gather_kernel,
        out_shape=[bf16(2, 4, TILE, HD), bf16(2, 3, TILE, HD)],
        in_specs=[ANY] * 3,
        out_specs=[VMEM] * 2,
        scratch_shapes=[pltpu.SemaphoreType.DMA((4,))],
        compiler_params=PARAMS,
        cost_estimate=cost(C_GATHER),
    )(kvx, kvm, ctx)


def attend_pairs(plan, count, off, bias, q, keys, values, peak, acc, bufs, at_step=None):
    score_a, score_b, weight_a, weight_b = bufs
    scale = LOG2E / HD**0.5

    def scored(i, scores):
        scores[...] = lax.dot_general(
            q[plan[0, i]], keys[plan[1, i]], (((1,), (1,)), ((), ())), preferred_element_type=jnp.float32
        )

    def weighed(i, scores, weights):
        at = plan[0, i]
        here = scores[...] * scale + (bias + off[i])
        old = peak[at]
        new = jnp.maximum(old, jnp.max(here, axis=1, keepdims=True))
        weights[...] = jnp.exp2(here - new[:, :1]).astype(jnp.bfloat16)
        shrink = jnp.exp2(old - new)
        peak[at] = new
        acc[at] = acc[at] * jnp.concatenate([shrink, shrink], axis=1)

    def added(i, weights):
        at = plan[0, i]
        acc[at] = acc[at] + jnp.dot(weights[...], values[plan[1, i]], preferred_element_type=jnp.float32)

    scored(0, score_a)
    weighed(0, score_a, weight_a)
    scored(1, score_b)

    def step(j, carry):
        if at_step is not None:
            at_step(j)
        i = 2 * j
        scored(i + 2, score_a)
        weighed(i + 1, score_b, weight_b)
        added(i, weight_a)
        scored(i + 3, score_b)
        weighed(i + 2, score_a, weight_a)
        added(i + 1, weight_b)
        return carry

    lax.fori_loop(0, lax.div(count + 1, 2), step, 0)


def plan_pairs(window, plan, off):
    count = 4 * window
    for back in range(WMAX):
        for frame in range(4):
            here = 4 * back + frame
            plan[0, here] = frame
            plan[1, here] = 3 + frame - back
            off[here] = 0.0
    for more in range(3):
        plan[0, count + more] = 0
        plan[1, count + more] = 3
        off[count + more] = -jnp.inf
    return count


def edge_bias(edges):
    cam, count = lax.axis_index("cam"), lax.axis_size("cam")
    left, right = edges[(cam + count - 1) % count], edges[cam]
    spot = lax.broadcasted_iota(jnp.int32, (1, 3 * TILE), 1)
    seen = (spot >= TILE - left * (TILE // 8)) & (spot < 2 * TILE + right * (TILE // 8))
    return jnp.where(seen, 0.0, -jnp.inf).astype(jnp.float32)


def started(pairs, sems):
    copies = [pltpu.make_async_copy(src, dst, sem) for (src, dst), sem in zip(pairs, sems)]
    for copy in copies:
        copy.start()
    return copies


PLACES = (1, 0, 2)


def attend_kernel(head, windows, edges, q_own, q_far, *refs):
    pieces, (out_own, out_far, q, keys, values, peak, acc, *bufs, plan, off, sems) = refs[:6], refs[6:]
    mine = x_low()
    pairs = [(q_own.at[head], q.at[pl.ds(2 * mine, 2)]), (q_far.at[head], q.at[pl.ds(2 - 2 * mine, 2)])]
    for n, (piece, frames) in enumerate(zip(pieces, [pl.ds(3, 4)] * 3 + [pl.ds(0, 3)] * 3)):
        rows = pl.ds(PLACES[n % 3] * TILE, TILE)
        pairs.append((piece.at[0], keys.at[frames, rows]))
        pairs.append((piece.at[1], values.at[frames, rows, pl.ds(0, HD)]))
    copies = started(pairs, [sems.at[i] for i in range(len(pairs))])
    values[:, :, HD:] = jnp.ones((values.shape[0], 3 * TILE, HD), jnp.bfloat16)
    acc[...] = jnp.zeros_like(acc)
    peak[...] = jnp.full_like(peak, -jnp.inf)
    count = plan_pairs(windows[PAIR * mine + head], plan, off)
    for copy in copies[:8]:
        copy.wait()

    def earlier(j):
        @pl.when(j == 1)
        def _():
            for copy in copies[8:]:
                copy.wait()

    attend_pairs(plan, count, off, edge_bias(edges), q, keys, values, peak, acc, bufs, earlier)
    for out, first in ((out_own, 2 * mine), (out_far, 2 - 2 * mine)):
        for n in range(2):
            done = acc[first + n]
            out[n] = (done[:, :HD] / done[:, HD:]).astype(jnp.bfloat16)


def attend(head, windows, edges, q_own, q_far, pieces):
    return pl.pallas_call(
        functools.partial(attend_kernel, head),
        out_shape=[bf16(2, TILE, HD)] * 2,
        in_specs=[SMEM, SMEM] + [ANY] * (2 + len(pieces)),
        out_specs=[VMEM] * 2,
        scratch_shapes=[
            pltpu.VMEM((4, TILE, HD), jnp.bfloat16),
            pltpu.VMEM((7, 3 * TILE, HD), jnp.bfloat16),
            pltpu.VMEM((7, 3 * TILE, 2 * HD), jnp.bfloat16),
            pltpu.VMEM((4, TILE, HD), jnp.float32),
            pltpu.VMEM((4, TILE, 2 * HD), jnp.float32),
            pltpu.VMEM((TILE, 3 * TILE), jnp.float32),
            pltpu.VMEM((TILE, 3 * TILE), jnp.float32),
            pltpu.VMEM((TILE, 3 * TILE), jnp.bfloat16),
            pltpu.VMEM((TILE, 3 * TILE), jnp.bfloat16),
            pltpu.SMEM((2, 4 * WMAX + 4), jnp.int32),
            pltpu.SMEM((4 * WMAX + 4,), jnp.float32),
            pltpu.SemaphoreType.DMA((14,)),
        ],
        compiler_params=PARAMS,
        cost_estimate=cost(C_ATTEND),
    )(windows, edges, q_own, q_far, *pieces)


def mix_kernel(*refs):
    pieces, (w_own, w_mine, w_core, out, held, w, made, sem_a, sem_o) = refs[:8], refs[8:]
    mine, core = x_low(), lax.axis_index("cam") % 2
    part = PAIR * HD
    width = w_own.shape[1]
    half = width // 2
    rows = lambda at: pl.ds(pl.multiple_of(at, part), part)
    inputs = started(
        [(piece, held.at[n % 4, :, :, pl.ds(n // 4 * HD, HD)]) for n, piece in enumerate(pieces)],
        [sem_a.at[i] for i in range(8)],
    )

    @pl.when(core == mine)
    def _():
        w[0], w[1] = w_mine[...], w_core[...]

    @pl.when(core != mine)
    def _():
        w[0], w[1] = w_core[...], w_mine[...]

    for copy in inputs:
        copy.wait()

    def group(first, weights, cols):
        total = None
        for n, weight in enumerate(weights):
            both = held[first + n].reshape(2 * TILE, part)
            term = jnp.dot(both, weight[:, cols], preferred_element_type=jnp.float32)
            total = term if total is None else total + term
        return total.astype(jnp.bfloat16).astype(jnp.float32)

    outs = []
    for n in range(2):
        cols = slice(n * half, (n + 1) * half)
        first = group(0, (w_own.at[rows(part * mine)], w_own.at[rows(part * (1 - mine))]), cols)
        second = group(2, (w.at[0], w.at[1]), cols)
        made[n] = (first + second).astype(jnp.bfloat16)
        outs += started([(made.at[n], out.at[:, pl.ds(n * half, half)])], [sem_o.at[n]])
    for copy in outs:
        copy.wait()


def mix(attended, w_own, w_mine, w_core):
    rows, width = 2 * TILE, w_own.shape[1]
    return pl.pallas_call(
        mix_kernel,
        out_shape=bf16(rows, width),
        in_specs=[ANY] * 8 + [VMEM] * 3,
        out_specs=ANY,
        scratch_shapes=[
            pltpu.VMEM((4, 2, TILE, PAIR * HD), jnp.bfloat16),
            pltpu.VMEM((2,) + w_mine.shape, jnp.bfloat16),
            pltpu.VMEM((2, rows, width // 2), jnp.bfloat16),
            pltpu.SemaphoreType.DMA((8,)),
            pltpu.SemaphoreType.DMA((2,)),
        ],
        compiler_params=pltpu.CompilerParams(vmem_limit_bytes=24 * MIB),
        cost_estimate=cost(C_MIX),
    )(*attended, w_own, w_mine, w_core)


def body(tokens, w_qkv, w_out, window_len, edge_counts, context_kv):
    frames, cols, row_count, width = tokens.shape
    sizes = tuple(lax.axis_size(axis) for axis in AXES)
    tm_count, cam_count, _ = sizes
    tm, cam, x_hi = (lax.axis_index(axis) for axis in AXES)
    x_lo, core = tm % 2, cam % 2

    def moved(move):
        pairs = pairs_of(sizes, move)
        return lambda shard: lax.ppermute(shard, AXES, pairs)

    to_mate = moved(lambda t, c, h: (t ^ 1, c, h))
    to_over = moved(lambda t, c, h: (t, c, 1 - h))
    to_diag = moved(lambda t, c, h: (t ^ 1, c, 1 - h))
    to_later = moved(lambda t, c, h: ((t + 2) % tm_count, c, h))
    to_right = moved(lambda t, c, h: (t, (c + 1) % cam_count, h))
    to_left = moved(lambda t, c, h: (t, (c - 1) % cam_count, h))
    to_core = moved(lambda t, c, h: (t, c ^ 1, h))
    wide = lambda shard: [shard, to_right(shard), to_left(shard)]

    flat = tokens.reshape(frames * cols * row_count, width)
    w3 = jnp.transpose(w_qkv, (1, 0, 2))
    kv_shape = bf16(1, 2, frames, TILE, HD)
    q_shape = bf16(PAIR, frames, TILE, HD)

    sent = project([(1, False, 0, (0,)), (2, False, 0, (1,))], [kv_shape] * 2, flat, w3, cost(C_SEND))
    kvx = [to_mate(one[0]) for one in sent]
    if not SPLIT:
        kvx = lax.optimization_barrier(kvx)

    def cached(context_kv):
        ctx = []
        for head in range(PAIR):
            part = lax.dynamic_slice_in_dim(context_kv, (PAIR * x_lo + head) * HD, HD, 4)
            ctx.append(jnp.transpose(part.reshape(WMAX - 1, TILE, 2, HD), (2, 0, 1, 3)))
        return ctx

    if CTX_FIRST:
        ctx = cached(lax.optimization_barrier((context_kv, sent))[0])
        flat, _ = lax.optimization_barrier((flat, ctx))
    else:
        flat, _ = lax.optimization_barrier((flat, sent))
    *kvm, q_sent, q_own = project(
        [(1, True, 0, (0,)), (2, True, 0, (1,)), (0, False, 2, ()), (0, True, 3, ())],
        [kv_shape] * 2 + [q_shape] * 2,
        flat,
        w3,
        cost(C_OWN),
    )
    if not CTX_FIRST:
        ctx = cached(lax.optimization_barrier((context_kv, q_own))[0])
    if Q_AFTER:
        q_sent, _ = lax.optimization_barrier((q_sent, kvx[Q_AFTER - 1]))
    q_far = to_mate(q_sent)

    four, halo = [], []
    for head in range(PAIR):
        one, later = gather(kvx[head], kvm[head][0], ctx[head])
        outer = one
        if head and OUTER_B == 1:
            outer, q_far, four[0] = lax.optimization_barrier((one, q_far, four[0]))
        if head and OUTER_B == 2:
            outer, halo[0] = lax.optimization_barrier((one, halo[0]))
        four.append([one, to_right(outer), to_left(outer)])
        halo.append(to_later(later))
        if head == 0 or OUTER_B != 3:
            halo[head] = wide(halo[head])
        else:
            later, four = lax.optimization_barrier((halo[1], four))
            halo[1] = wide(later)

    half = w_out.shape[1] // 2

    def fetched(w_out):
        w_part = lax.dynamic_slice(w_out, (core * PAIR * HD, (1 - x_hi) * half), (PAIR * HD, half))
        return to_diag(w_part)

    if W_AFTER == 0:
        w_mine = fetched(w_out)
    if W_AFTER == 1:
        w_mine = fetched(lax.optimization_barrier((w_out, four[1][0]))[0])
    if W_AFTER == 2:
        w_now, four[1] = lax.optimization_barrier((w_out, four[1]))
        w_mine = fetched(w_now)
    if W_AFTER == 3:
        w_now, halo[0] = lax.optimization_barrier((w_out, halo[0]))
        w_mine = fetched(w_now)

    pieces = []
    for head in range(PAIR):
        own, mates = attend(head, window_len, edge_counts, q_own, q_far, four[head] + halo[head])
        if head:
            if EXCH:
                own, mates, pieces = lax.optimization_barrier((own, mates, pieces))
        else:
            if W_AFTER == 4:
                w_mine = fetched(lax.optimization_barrier((w_out, own))[0])
            else:
                w_mine, _ = lax.optimization_barrier((w_mine, own))
            w_core = to_core(w_mine)
            w_own = lax.dynamic_slice_in_dim(lax.optimization_barrier((w_out, own))[0], x_hi * half, half, 1)
        pieces.append([own, to_mate(mates), to_over(own), to_diag(mates)])
    out = mix(pieces[0] + pieces[1], w_own, w_mine, w_core)
    return out.reshape(frames, cols, row_count, -1)


def solution(mesh):
    placed = (
        P("tm", "cam", None, None),
        P(None, None, "head"),
        P("head", None),
        P("head"),
        P(),
        P(None, "cam", None, None, "head"),
    )
    return jax.shard_map(
        body, mesh=mesh, in_specs=placed, out_specs=P("tm", "cam", None, "head"), check_vma=False
    )
```

```python
import functools

import jax
import jax.numpy as jnp
from jax import lax
from jax.experimental import pallas as pl
from jax.experimental.pallas import tpu as pltpu
from jax.sharding import PartitionSpec as P

AXES = ("tm", "cam", "head")
HD = 128
WMAX = 4
PAIR = 2
TILE = 256
LOG2E = 1.4426950408889634
MIB = 1 << 20
ANY = pl.BlockSpec(memory_space=pl.ANY)
VMEM = pl.BlockSpec(memory_space=pltpu.VMEM)
SMEM = pl.BlockSpec(memory_space=pltpu.SMEM)
PARAMS = pltpu.CompilerParams(vmem_limit_bytes=64 * MIB)
SMALL = pl.CostEstimate(flops=10**9, bytes_accessed=1000, transcendentals=0)


def pairs_of(sizes, move):
    tm, cam, head = sizes
    flat = lambda t, c, h: (t * cam + c) * head + h
    return [
        (flat(t, c, h), flat(*move(t, c, h)))
        for t in range(tm)
        for c in range(cam)
        for h in range(head)
    ]


def x_low():
    return lax.axis_index("tm") % 2


def bf16(*shape):
    return jax.ShapeDtypeStruct(shape, jnp.bfloat16)


def project_kernel(blocks, chunks, tokens, w3, *refs):
    outs, (flat, w, sem_t, sem_w) = refs[:-4], refs[-4:]
    mine = x_low()
    depth = flat.shape[1] // chunks
    steps = []
    for k in range(chunks):
        ks = pl.ds(k * depth, depth)
        copies = [pltpu.make_async_copy(tokens.at[:, ks], flat.at[:, ks], sem_t.at[k])]
        for i, (which, own, _, _) in enumerate(blocks):
            col = pl.multiple_of(PAIR * HD * (mine if own else 1 - mine), PAIR * HD)
            copies.append(
                pltpu.make_async_copy(
                    w3.at[which, ks, pl.ds(col, PAIR * HD)],
                    w.at[ks, pl.ds(i * PAIR * HD, PAIR * HD)],
                    sem_w.at[k, i],
                )
            )
        steps.append(copies)
        for copy in copies:
            copy.start()
    total = None
    for k, copies in enumerate(steps):
        for copy in copies:
            copy.wait()
        ks = slice(k * depth, (k + 1) * depth)
        made = jnp.dot(flat[:, ks], w[ks, :], preferred_element_type=jnp.float32)
        total = made if total is None else total + made
    total = total.astype(jnp.bfloat16)
    for i, (_, _, out, at) in enumerate(blocks):
        for head in range(PAIR):
            col = (i * PAIR + head) * HD
            piece = total[:, col : col + HD].reshape(-1, TILE, HD)
            if at:
                outs[out + head][(0,) + at] = piece
            else:
                outs[out][head] = piece


def project(blocks, shapes, tokens, w3):
    rows, width = tokens.shape
    chunks = 4
    return pl.pallas_call(
        functools.partial(project_kernel, blocks, chunks),
        out_shape=shapes,
        in_specs=[ANY, ANY],
        out_specs=[VMEM] * len(shapes),
        scratch_shapes=[
            pltpu.VMEM((rows, width), jnp.bfloat16),
            pltpu.VMEM((width, len(blocks) * PAIR * HD), jnp.bfloat16),
            pltpu.SemaphoreType.DMA((chunks,)),
            pltpu.SemaphoreType.DMA((chunks, len(blocks))),
        ],
        compiler_params=PARAMS,
        cost_estimate=SMALL,
    )(tokens, w3)


def run_copies(pairs, sems):
    copies = [pltpu.make_async_copy(src, dst, sems.at[i]) for i, (src, dst) in enumerate(pairs)]
    for copy in copies:
        copy.start()
    for copy in copies:
        copy.wait()


def gather_kernel(kvx, kvm, ctx, four, halo, sems):
    tm, count = lax.axis_index("tm"), lax.axis_size("tm")
    mine = tm % 2
    pairs = [(kvm, four.at[:, pl.ds(2 * mine, 2)]), (kvx, four.at[:, pl.ds(2 - 2 * mine, 2)])]

    @pl.when(tm >= count - 2)
    def _():
        run_copies(pairs + [(ctx, halo)], sems)

    @pl.when((tm < count - 2) & (mine == 0))
    def _():
        run_copies(pairs + [(kvm.at[:, 1], halo.at[:, 0]), (kvx, halo.at[:, pl.ds(1, 2)])], sems)

    @pl.when((tm < count - 2) & (mine == 1))
    def _():
        run_copies(pairs + [(kvx.at[:, 1], halo.at[:, 0]), (kvm, halo.at[:, pl.ds(1, 2)])], sems)


def gather(kvx, kvm, ctx):
    return pl.pallas_call(
        gather_kernel,
        out_shape=[bf16(2, 4, TILE, HD), bf16(2, 3, TILE, HD)],
        in_specs=[ANY] * 3,
        out_specs=[VMEM] * 2,
        scratch_shapes=[pltpu.SemaphoreType.DMA((4,))],
        compiler_params=PARAMS,
        cost_estimate=SMALL,
    )(kvx, kvm, ctx)


def attend_pairs(plan, count, off, bias, q, keys, values, peak, acc, bufs, at_step=None):
    score_a, score_b, weight_a, weight_b = bufs
    scale = LOG2E / HD**0.5

    def scored(i, scores):
        scores[...] = lax.dot_general(
            q[plan[0, i]], keys[plan[1, i]], (((1,), (1,)), ((), ())), preferred_element_type=jnp.float32
        )

    def weighed(i, scores, weights):
        at = plan[0, i]
        here = scores[...] * scale + (bias + off[i])
        old = peak[at]
        new = jnp.maximum(old, jnp.max(here, axis=1, keepdims=True))
        weights[...] = jnp.exp2(here - new[:, :1]).astype(jnp.bfloat16)
        shrink = jnp.exp2(old - new)
        peak[at] = new
        acc[at] = acc[at] * jnp.concatenate([shrink, shrink], axis=1)

    def added(i, weights):
        at = plan[0, i]
        acc[at] = acc[at] + jnp.dot(weights[...], values[plan[1, i]], preferred_element_type=jnp.float32)

    scored(0, score_a)
    weighed(0, score_a, weight_a)
    scored(1, score_b)

    def step(j, carry):
        if at_step is not None:
            at_step(j)
        i = 2 * j
        scored(i + 2, score_a)
        weighed(i + 1, score_b, weight_b)
        added(i, weight_a)
        scored(i + 3, score_b)
        weighed(i + 2, score_a, weight_a)
        added(i + 1, weight_b)
        return carry

    lax.fori_loop(0, lax.div(count + 1, 2), step, 0)


def plan_pairs(window, plan, off):
    count = 4 * window
    for back in range(WMAX):
        for frame in range(4):
            here = 4 * back + frame
            plan[0, here] = frame
            plan[1, here] = 3 + frame - back
            off[here] = 0.0
    for more in range(3):
        plan[0, count + more] = 0
        plan[1, count + more] = 3
        off[count + more] = -jnp.inf
    return count


def edge_bias(edges):
    cam, count = lax.axis_index("cam"), lax.axis_size("cam")
    left, right = edges[(cam + count - 1) % count], edges[cam]
    spot = lax.broadcasted_iota(jnp.int32, (1, 3 * TILE), 1)
    seen = (spot >= TILE - left * (TILE // 8)) & (spot < 2 * TILE + right * (TILE // 8))
    return jnp.where(seen, 0.0, -jnp.inf).astype(jnp.float32)


def started(pairs, sems):
    copies = [pltpu.make_async_copy(src, dst, sem) for (src, dst), sem in zip(pairs, sems)]
    for copy in copies:
        copy.start()
    return copies


PLACES = (1, 0, 2)


def attend_kernel(head, windows, edges, q_own, q_far, *refs):
    pieces, (out_own, out_far, q, keys, values, peak, acc, *bufs, plan, off, sems) = refs[:6], refs[6:]
    mine = x_low()
    pairs = [(q_own.at[head], q.at[pl.ds(2 * mine, 2)]), (q_far.at[head], q.at[pl.ds(2 - 2 * mine, 2)])]
    for n, (piece, frames) in enumerate(zip(pieces, [pl.ds(3, 4)] * 3 + [pl.ds(0, 3)] * 3)):
        rows = pl.ds(PLACES[n % 3] * TILE, TILE)
        pairs.append((piece.at[0], keys.at[frames, rows]))
        pairs.append((piece.at[1], values.at[frames, rows, pl.ds(0, HD)]))
    copies = started(pairs, [sems.at[i] for i in range(len(pairs))])
    values[:, :, HD:] = jnp.ones((values.shape[0], 3 * TILE, HD), jnp.bfloat16)
    acc[...] = jnp.zeros_like(acc)
    peak[...] = jnp.full_like(peak, -jnp.inf)
    count = plan_pairs(windows[PAIR * mine + head], plan, off)
    for copy in copies[:8]:
        copy.wait()

    def earlier(j):
        @pl.when(j == 1)
        def _():
            for copy in copies[8:]:
                copy.wait()

    attend_pairs(plan, count, off, edge_bias(edges), q, keys, values, peak, acc, bufs, earlier)
    for out, first in ((out_own, 2 * mine), (out_far, 2 - 2 * mine)):
        for n in range(2):
            done = acc[first + n]
            out[n] = (done[:, :HD] / done[:, HD:]).astype(jnp.bfloat16)


def attend(head, windows, edges, q_own, q_far, pieces):
    return pl.pallas_call(
        functools.partial(attend_kernel, head),
        out_shape=[bf16(2, TILE, HD)] * 2,
        in_specs=[SMEM, SMEM] + [ANY] * (2 + len(pieces)),
        out_specs=[VMEM] * 2,
        scratch_shapes=[
            pltpu.VMEM((4, TILE, HD), jnp.bfloat16),
            pltpu.VMEM((7, 3 * TILE, HD), jnp.bfloat16),
            pltpu.VMEM((7, 3 * TILE, 2 * HD), jnp.bfloat16),
            pltpu.VMEM((4, TILE, HD), jnp.float32),
            pltpu.VMEM((4, TILE, 2 * HD), jnp.float32),
            pltpu.VMEM((TILE, 3 * TILE), jnp.float32),
            pltpu.VMEM((TILE, 3 * TILE), jnp.float32),
            pltpu.VMEM((TILE, 3 * TILE), jnp.bfloat16),
            pltpu.VMEM((TILE, 3 * TILE), jnp.bfloat16),
            pltpu.SMEM((2, 4 * WMAX + 4), jnp.int32),
            pltpu.SMEM((4 * WMAX + 4,), jnp.float32),
            pltpu.SemaphoreType.DMA((14,)),
        ],
        compiler_params=PARAMS,
        cost_estimate=SMALL,
    )(windows, edges, q_own, q_far, *pieces)


def mix_kernel(*refs):
    pieces, (w_out, w_mine, w_core, out, first, second, w, made, sem_a, sem_w, sem_o) = refs[:8], refs[8:]
    mine, core, head = x_low(), lax.axis_index("cam") % 2, lax.axis_index("head")
    part = PAIR * HD
    width = w.shape[1]
    half = width // 2
    rows = lambda at: pl.ds(pl.multiple_of(at, part), part)
    pairs = []
    for n, piece in enumerate(pieces):
        held = (first, second)[n // 4]
        pairs.append((piece, held.at[:, :, pl.ds(n % 4 * HD, HD)]))
    inputs = started(pairs, [sem_a.at[i] for i in range(8)])
    weights = []
    for n in range(2):
        cols = pl.ds(n * half, half)
        there = pl.ds(pl.multiple_of(head * width + n * half, half), half)
        pairs = [
            (w_out.at[rows(part * mine), there], w.at[pl.ds(0, part), cols]),
            (w_out.at[rows(part * (1 - mine)), there], w.at[pl.ds(part, part), cols]),
            (w_mine.at[:, cols], w.at[rows(jnp.where(core == mine, 2, 3) * part), cols]),
            (w_core.at[:, cols], w.at[rows(jnp.where(core == mine, 3, 2) * part), cols]),
        ]
        weights.append(started(pairs, [sem_w.at[n, i] for i in range(4)]))
    for copy in inputs:
        copy.wait()

    def group(held, at, cols):
        total = jnp.dot(
            held[...].reshape(2 * TILE, 2 * part), w[at : at + 2 * part, cols], preferred_element_type=jnp.float32
        )
        return total.astype(jnp.bfloat16).astype(jnp.float32)

    outs = []
    for n in range(2):
        for copy in weights[n]:
            copy.wait()
        cols = slice(n * half, (n + 1) * half)
        made[n] = (group(first, 0, cols) + group(second, 2 * part, cols)).astype(jnp.bfloat16)
        outs += started([(made.at[n], out.at[:, pl.ds(n * half, half)])], [sem_o.at[n]])
    for copy in outs:
        copy.wait()


def mix(attended, w_out, w_mine, w_core):
    rows = 2 * TILE
    width = w_out.shape[1] // 2
    return pl.pallas_call(
        mix_kernel,
        out_shape=bf16(rows, width),
        in_specs=[ANY] * 11,
        out_specs=ANY,
        scratch_shapes=[
            pltpu.VMEM((2, TILE, 2 * PAIR * HD), jnp.bfloat16),
            pltpu.VMEM((2, TILE, 2 * PAIR * HD), jnp.bfloat16),
            pltpu.VMEM((4 * PAIR * HD, width), jnp.bfloat16),
            pltpu.VMEM((2, rows, width // 2), jnp.bfloat16),
            pltpu.SemaphoreType.DMA((8,)),
            pltpu.SemaphoreType.DMA((2, 4)),
            pltpu.SemaphoreType.DMA((2,)),
        ],
        compiler_params=PARAMS,
        cost_estimate=SMALL,
    )(*attended, w_out, w_mine, w_core)


def body(tokens, w_qkv, w_out, window_len, edge_counts, context_kv):
    frames, cols, row_count, width = tokens.shape
    sizes = tuple(lax.axis_size(axis) for axis in AXES)
    tm_count, cam_count, _ = sizes
    tm, cam, x_hi = (lax.axis_index(axis) for axis in AXES)
    x_lo, core = tm % 2, cam % 2

    def moved(move):
        pairs = pairs_of(sizes, move)
        return lambda shard: lax.ppermute(shard, AXES, pairs)

    to_mate = moved(lambda t, c, h: (t ^ 1, c, h))
    to_over = moved(lambda t, c, h: (t, c, 1 - h))
    to_diag = moved(lambda t, c, h: (t ^ 1, c, 1 - h))
    to_later = moved(lambda t, c, h: ((t + 2) % tm_count, c, h))
    to_right = moved(lambda t, c, h: (t, (c + 1) % cam_count, h))
    to_left = moved(lambda t, c, h: (t, (c - 1) % cam_count, h))
    to_core = moved(lambda t, c, h: (t, c ^ 1, h))
    wide = lambda shard: [shard, to_right(shard), to_left(shard)]

    flat = tokens.reshape(frames * cols * row_count, width)
    w3 = jnp.transpose(w_qkv, (1, 0, 2))
    kv_shape = bf16(1, 2, frames, TILE, HD)
    q_shape = bf16(PAIR, frames, TILE, HD)

    sent = project([(1, False, 0, (0,)), (2, False, 0, (1,))], [kv_shape] * 2, flat, w3)
    hold = lambda x, *after: lax.optimization_barrier((x, after))[0]
    kvx = [to_mate(sent[0][0])]
    *kvm, q_sent, q_own = project(
        [(1, True, 0, (0,)), (2, True, 0, (1,)), (0, False, 2, ()), (0, True, 3, ())],
        [kv_shape] * 2 + [q_shape] * 2,
        hold(flat, sent),
        w3,
    )
    kvx.append(to_mate(hold(sent[1], q_own)[0]))
    q_far = to_mate(hold(q_sent, kvx[1]))

    four, later = [], []
    for head in range(PAIR):
        ctx = lax.dynamic_slice_in_dim(hold(context_kv, q_own), (PAIR * x_lo + head) * HD, HD, 4)
        ctx = jnp.transpose(ctx.reshape(WMAX - 1, TILE, 2, HD), (2, 0, 1, 3))
        one, halo = gather(kvx[head], kvm[head][0], ctx)
        later.append(to_later(halo))
        outer = hold(one, four[0], q_far) if head else one
        four.append([one, to_right(outer), to_left(outer)])
    halo = [wide(one) for one in later]

    half = w_out.shape[1] // 2
    w_part = lax.dynamic_slice(
        hold(w_out, four[0][0]), (core * PAIR * HD, (1 - x_hi) * half), (PAIR * HD, half)
    )
    w_mine = to_diag(w_part)

    pieces = []
    for head in range(PAIR):
        mine, mates = attend(head, window_len, edge_counts, q_own, q_far, four[head] + halo[head])
        if head == 0:
            w_core = to_core(hold(w_mine, mine))
        else:
            mine, mates, pieces = lax.optimization_barrier((mine, mates, pieces))
        pieces.append([mine, to_mate(mates), to_over(mine), to_diag(mates)])
    attended = [piece for both in zip(*pieces) for piece in both]
    out = mix(attended, w_out, w_mine, w_core)
    return out.reshape(frames, cols, row_count, -1)


def solution(mesh):
    placed = (
        P("tm", "cam", None, None),
        P(None, None, "head"),
        P("head", None),
        P("head"),
        P(),
        P(None, "cam", None, None, "head"),
    )
    return jax.shard_map(
        body, mesh=mesh, in_specs=placed, out_specs=P("tm", "cam", None, "head"), check_vma=False
    )
```

```python
import functools

import jax
import jax.numpy as jnp
from jax import lax
from jax.experimental import pallas as pl
from jax.experimental.pallas import tpu as pltpu
from jax.sharding import PartitionSpec as P

AXES = ("tm", "cam", "head")
HD = 128
WMAX = 4
PAIR = 2
TILE = 256
LOG2E = 1.4426950408889634
MIB = 1 << 20
ANY = pl.BlockSpec(memory_space=pl.ANY)
VMEM = pl.BlockSpec(memory_space=pltpu.VMEM)
SMEM = pl.BlockSpec(memory_space=pltpu.SMEM)
PARAMS = pltpu.CompilerParams(vmem_limit_bytes=64 * MIB)
SMALL = pl.CostEstimate(flops=10**9, bytes_accessed=1000, transcendentals=0)


def pairs_of(sizes, move):
    tm, cam, head = sizes
    flat = lambda t, c, h: (t * cam + c) * head + h
    return [
        (flat(t, c, h), flat(*move(t, c, h)))
        for t in range(tm)
        for c in range(cam)
        for h in range(head)
    ]


def x_low():
    return lax.axis_index("tm") % 2


def bf16(*shape):
    return jax.ShapeDtypeStruct(shape, jnp.bfloat16)


def project_kernel(blocks, chunks, tokens, w3, *refs):
    outs, (flat, w, sem_t, sem_w) = refs[:-4], refs[-4:]
    mine = x_low()
    depth = flat.shape[1] // chunks
    steps = []
    for k in range(chunks):
        ks = pl.ds(k * depth, depth)
        copies = [pltpu.make_async_copy(tokens.at[:, ks], flat.at[:, ks], sem_t.at[k])]
        for i, (which, own, _, _) in enumerate(blocks):
            col = pl.multiple_of(PAIR * HD * (mine if own else 1 - mine), PAIR * HD)
            copies.append(
                pltpu.make_async_copy(
                    w3.at[which, ks, pl.ds(col, PAIR * HD)],
                    w.at[ks, pl.ds(i * PAIR * HD, PAIR * HD)],
                    sem_w.at[k, i],
                )
            )
        steps.append(copies)
        for copy in copies:
            copy.start()
    total = None
    for k, copies in enumerate(steps):
        for copy in copies:
            copy.wait()
        ks = slice(k * depth, (k + 1) * depth)
        made = jnp.dot(flat[:, ks], w[ks, :], preferred_element_type=jnp.float32)
        total = made if total is None else total + made
    total = total.astype(jnp.bfloat16)
    for i, (_, _, out, at) in enumerate(blocks):
        for head in range(PAIR):
            col = (i * PAIR + head) * HD
            piece = total[:, col : col + HD].reshape(-1, TILE, HD)
            if at:
                outs[out + head][(0,) + at] = piece
            else:
                outs[out][head] = piece


def project(blocks, shapes, tokens, w3):
    rows, width = tokens.shape
    chunks = 4
    return pl.pallas_call(
        functools.partial(project_kernel, blocks, chunks),
        out_shape=shapes,
        in_specs=[ANY, ANY],
        out_specs=[VMEM] * len(shapes),
        scratch_shapes=[
            pltpu.VMEM((rows, width), jnp.bfloat16),
            pltpu.VMEM((width, len(blocks) * PAIR * HD), jnp.bfloat16),
            pltpu.SemaphoreType.DMA((chunks,)),
            pltpu.SemaphoreType.DMA((chunks, len(blocks))),
        ],
        compiler_params=PARAMS,
        cost_estimate=SMALL,
    )(tokens, w3)


def run_copies(pairs, sems):
    copies = [pltpu.make_async_copy(src, dst, sems.at[i]) for i, (src, dst) in enumerate(pairs)]
    for copy in copies:
        copy.start()
    for copy in copies:
        copy.wait()


def gather_kernel(kvx, kvm, four, halo, sems):
    mine = x_low()
    pairs = [(kvm, four.at[:, pl.ds(2 * mine, 2)]), (kvx, four.at[:, pl.ds(2 - 2 * mine, 2)])]

    @pl.when(mine == 0)
    def _():
        run_copies(pairs + [(kvm.at[:, 1], halo.at[:, 0]), (kvx, halo.at[:, pl.ds(1, 2)])], sems)

    @pl.when(mine == 1)
    def _():
        run_copies(pairs + [(kvx.at[:, 1], halo.at[:, 0]), (kvm, halo.at[:, pl.ds(1, 2)])], sems)


def gather(kvx, kvm):
    return pl.pallas_call(
        gather_kernel,
        out_shape=[bf16(2, 4, TILE, HD), bf16(2, 3, TILE, HD)],
        in_specs=[ANY] * 2,
        out_specs=[VMEM] * 2,
        scratch_shapes=[pltpu.SemaphoreType.DMA((4,))],
        compiler_params=PARAMS,
        cost_estimate=SMALL,
    )(kvx, kvm)


def attend_pairs(plan, count, off, bias, q, keys, values, peak, acc, bufs, at_step=None):
    score_a, score_b, weight_a, weight_b = bufs
    scale = LOG2E / HD**0.5

    def scored(i, scores):
        scores[...] = lax.dot_general(
            q[plan[0, i]], keys[plan[1, i]], (((1,), (1,)), ((), ())), preferred_element_type=jnp.float32
        )

    def weighed(i, scores, weights):
        at = plan[0, i]
        here = scores[...] * scale + (bias + off[i])
        old = peak[at]
        new = jnp.maximum(old, jnp.max(here, axis=1, keepdims=True))
        weights[...] = jnp.exp2(here - new[:, :1]).astype(jnp.bfloat16)
        shrink = jnp.exp2(old - new)
        peak[at] = new
        acc[at] = acc[at] * jnp.concatenate([shrink, shrink], axis=1)

    def added(i, weights):
        at = plan[0, i]
        acc[at] = acc[at] + jnp.dot(weights[...], values[plan[1, i]], preferred_element_type=jnp.float32)

    scored(0, score_a)
    weighed(0, score_a, weight_a)
    scored(1, score_b)

    def step(j, carry):
        if at_step is not None:
            at_step(j)
        i = 2 * j
        scored(i + 2, score_a)
        weighed(i + 1, score_b, weight_b)
        added(i, weight_a)
        scored(i + 3, score_b)
        weighed(i + 2, score_a, weight_a)
        added(i + 1, weight_b)
        return carry

    lax.fori_loop(0, lax.div(count + 1, 2), step, 0)


def plan_pairs(window, plan, off):
    count = 4 * window
    for back in range(WMAX):
        for frame in range(4):
            here = 4 * back + frame
            plan[0, here] = frame
            plan[1, here] = 3 + frame - back
            off[here] = 0.0
    for more in range(3):
        plan[0, count + more] = 0
        plan[1, count + more] = 3
        off[count + more] = -jnp.inf
    return count


def edge_bias(edges):
    cam, count = lax.axis_index("cam"), lax.axis_size("cam")
    left, right = edges[(cam + count - 1) % count], edges[cam]
    spot = lax.broadcasted_iota(jnp.int32, (1, 3 * TILE), 1)
    seen = (spot >= TILE - left * (TILE // 8)) & (spot < 2 * TILE + right * (TILE // 8))
    return jnp.where(seen, 0.0, -jnp.inf).astype(jnp.float32)


def started(pairs, sems):
    copies = [pltpu.make_async_copy(src, dst, sem) for (src, dst), sem in zip(pairs, sems)]
    for copy in copies:
        copy.start()
    return copies


PLACES = (1, 0, 2)


def attend_kernel(head, windows, edges, q_own, q_far, *refs):
    pieces, (out_own, out_far, q, keys, values, peak, acc, *bufs, plan, off, sems) = refs[:6], refs[6:]
    mine = x_low()
    pairs = [(q_own.at[head], q.at[pl.ds(2 * mine, 2)]), (q_far.at[head], q.at[pl.ds(2 - 2 * mine, 2)])]
    for n, (piece, frames) in enumerate(zip(pieces, [pl.ds(3, 4)] * 3 + [pl.ds(0, 3)] * 3)):
        rows = pl.ds(PLACES[n % 3] * TILE, TILE)
        pairs.append((piece.at[0], keys.at[frames, rows]))
        pairs.append((piece.at[1], values.at[frames, rows, pl.ds(0, HD)]))
    copies = started(pairs, [sems.at[i] for i in range(len(pairs))])
    values[:, :, HD:] = jnp.ones((values.shape[0], 3 * TILE, HD), jnp.bfloat16)
    acc[...] = jnp.zeros_like(acc)
    peak[...] = jnp.full_like(peak, -jnp.inf)
    count = plan_pairs(windows[PAIR * mine + head], plan, off)
    for copy in copies[:8]:
        copy.wait()

    def earlier(j):
        @pl.when(j == 1)
        def _():
            for copy in copies[8:]:
                copy.wait()

    attend_pairs(plan, count, off, edge_bias(edges), q, keys, values, peak, acc, bufs, earlier)
    for out, first in ((out_own, 2 * mine), (out_far, 2 - 2 * mine)):
        for n in range(2):
            done = acc[first + n]
            out[n] = (done[:, :HD] / done[:, HD:]).astype(jnp.bfloat16)


def attend(head, windows, edges, q_own, q_far, pieces):
    return pl.pallas_call(
        functools.partial(attend_kernel, head),
        out_shape=[bf16(2, TILE, HD)] * 2,
        in_specs=[SMEM, SMEM] + [ANY] * (2 + len(pieces)),
        out_specs=[VMEM] * 2,
        scratch_shapes=[
            pltpu.VMEM((4, TILE, HD), jnp.bfloat16),
            pltpu.VMEM((7, 3 * TILE, HD), jnp.bfloat16),
            pltpu.VMEM((7, 3 * TILE, 2 * HD), jnp.bfloat16),
            pltpu.VMEM((4, TILE, HD), jnp.float32),
            pltpu.VMEM((4, TILE, 2 * HD), jnp.float32),
            pltpu.VMEM((TILE, 3 * TILE), jnp.float32),
            pltpu.VMEM((TILE, 3 * TILE), jnp.float32),
            pltpu.VMEM((TILE, 3 * TILE), jnp.bfloat16),
            pltpu.VMEM((TILE, 3 * TILE), jnp.bfloat16),
            pltpu.SMEM((2, 4 * WMAX + 4), jnp.int32),
            pltpu.SMEM((4 * WMAX + 4,), jnp.float32),
            pltpu.SemaphoreType.DMA((14,)),
        ],
        compiler_params=PARAMS,
        cost_estimate=SMALL,
    )(windows, edges, q_own, q_far, *pieces)


def mix_kernel(*refs):
    pieces, (w_out, w_mine, w_core, out, first, second, w, made, sem_a, sem_w, sem_o) = refs[:8], refs[8:]
    mine, core, head = x_low(), lax.axis_index("cam") % 2, lax.axis_index("head")
    part = PAIR * HD
    width = w.shape[1]
    half = width // 2
    rows = lambda at: pl.ds(pl.multiple_of(at, part), part)
    pairs = []
    for n, piece in enumerate(pieces):
        kind = n % 4
        held = (first, second)[kind // 2]
        pairs.append((piece, held.at[:, :, pl.ds((kind % 2 * PAIR + n // 4) * HD, HD)]))
    inputs = started(pairs, [sem_a.at[i] for i in range(8)])
    weights = []
    for n in range(2):
        cols = pl.ds(n * half, half)
        there = pl.ds(pl.multiple_of(head * width + n * half, half), half)
        pairs = [
            (w_out.at[rows(part * mine), there], w.at[pl.ds(0, part), cols]),
            (w_out.at[rows(part * (1 - mine)), there], w.at[pl.ds(part, part), cols]),
            (w_mine.at[:, cols], w.at[rows(jnp.where(core == mine, 2, 3) * part), cols]),
            (w_core.at[:, cols], w.at[rows(jnp.where(core == mine, 3, 2) * part), cols]),
        ]
        weights.append(started(pairs, [sem_w.at[n, i] for i in range(4)]))
    for copy in inputs:
        copy.wait()

    def group(held, at, cols):
        total = jnp.dot(
            held[...].reshape(2 * TILE, 2 * part), w[at : at + 2 * part, cols], preferred_element_type=jnp.float32
        )
        return total.astype(jnp.bfloat16).astype(jnp.float32)

    outs = []
    for n in range(2):
        for copy in weights[n]:
            copy.wait()
        cols = slice(n * half, (n + 1) * half)
        made[n] = (group(first, 0, cols) + group(second, 2 * part, cols)).astype(jnp.bfloat16)
        outs += started([(made.at[n], out.at[:, pl.ds(n * half, half)])], [sem_o.at[n]])
    for copy in outs:
        copy.wait()


def mix(attended, w_out, w_mine, w_core):
    rows = 2 * TILE
    width = w_out.shape[1] // 2
    return pl.pallas_call(
        mix_kernel,
        out_shape=bf16(rows, width),
        in_specs=[ANY] * 11,
        out_specs=ANY,
        scratch_shapes=[
            pltpu.VMEM((2, TILE, 2 * PAIR * HD), jnp.bfloat16),
            pltpu.VMEM((2, TILE, 2 * PAIR * HD), jnp.bfloat16),
            pltpu.VMEM((4 * PAIR * HD, width), jnp.bfloat16),
            pltpu.VMEM((2, rows, width // 2), jnp.bfloat16),
            pltpu.SemaphoreType.DMA((8,)),
            pltpu.SemaphoreType.DMA((2, 4)),
            pltpu.SemaphoreType.DMA((2,)),
        ],
        compiler_params=PARAMS,
        cost_estimate=SMALL,
    )(*attended, w_out, w_mine, w_core)


def body(tokens, w_qkv, w_out, window_len, edge_counts, context_kv):
    frames, cols, row_count, width = tokens.shape
    sizes = tuple(lax.axis_size(axis) for axis in AXES)
    tm_count, cam_count, _ = sizes
    tm, cam, x_hi = (lax.axis_index(axis) for axis in AXES)
    x_lo, core = tm % 2, cam % 2

    def moved(move):
        pairs = pairs_of(sizes, move)
        return lambda shard: lax.ppermute(shard, AXES, pairs)

    to_mate = moved(lambda t, c, h: (t ^ 1, c, h))
    to_over = moved(lambda t, c, h: (t, c, 1 - h))
    to_diag = moved(lambda t, c, h: (t ^ 1, c, 1 - h))
    to_later = moved(lambda t, c, h: ((t + 2) % tm_count, c, h))
    to_right = moved(lambda t, c, h: (t, (c + 1) % cam_count, h))
    to_left = moved(lambda t, c, h: (t, (c - 1) % cam_count, h))
    to_core = moved(lambda t, c, h: (t, c ^ 1, h))
    wide = lambda shard: [shard, to_right(shard), to_left(shard)]

    flat = tokens.reshape(frames * cols * row_count, width)
    w3 = jnp.transpose(w_qkv, (1, 0, 2))
    kv_shape = bf16(1, 2, frames, TILE, HD)
    q_shape = bf16(PAIR, frames, TILE, HD)

    sent = project([(1, False, 0, (0,)), (2, False, 0, (1,))], [kv_shape] * 2, flat, w3)
    hold = lambda x, *after: lax.optimization_barrier((x, after))[0]
    kvx = [to_mate(sent[0][0])]
    *kvm, q_sent, q_own = project(
        [(1, True, 0, (0,)), (2, True, 0, (1,)), (0, False, 2, ()), (0, True, 3, ())],
        [kv_shape] * 2 + [q_shape] * 2,
        hold(flat, sent),
        w3,
    )
    kvx.append(to_mate(hold(sent[1], q_own)[0]))
    q_far = to_mate(hold(q_sent, kvx[0]))

    four, later = [], []
    for head in range(PAIR):
        one, halo = gather(kvx[head], kvm[head][0])
        later.append(to_later(halo))
        outer = hold(one, four[0]) if head else one
        four.append([one, to_right(outer), to_left(outer)])
    halo = []
    for head in range(PAIR):
        ctx = lax.dynamic_slice_in_dim(hold(context_kv, four[1][0]), (PAIR * x_lo + head) * HD, HD, 4)
        ctx = jnp.transpose(ctx.reshape(WMAX - 1, TILE, 2, HD), (2, 0, 1, 3))
        halo.append(wide(jnp.where(tm < 2, ctx, hold(later[head], ctx))))

    half = w_out.shape[1] // 2
    w_part = lax.dynamic_slice(
        hold(w_out, four[0]), (core * PAIR * HD, (1 - x_hi) * half), (PAIR * HD, half)
    )
    w_mine = to_diag(w_part)

    pieces = []
    for head in range(PAIR):
        mine, mates = attend(head, window_len, edge_counts, q_own, q_far, four[head] + halo[head])
        if head == 0:
            w_core = to_core(hold(w_mine, mine))
        else:
            mine, mates, pieces = lax.optimization_barrier((mine, mates, pieces))
        pieces.append([mine, to_mate(mates), to_over(mine), to_diag(mates)])
    out = mix(pieces[0] + pieces[1], w_out, w_mine, w_core)
    return out.reshape(frames, cols, row_count, -1)


def solution(mesh):
    placed = (
        P("tm", "cam", None, None),
        P(None, None, "head"),
        P("head", None),
        P("head"),
        P(),
        P(None, "cam", None, None, "head"),
    )
    return jax.shard_map(
        body, mesh=mesh, in_specs=placed, out_specs=P("tm", "cam", None, "head"), check_vma=False
    )
```

```python
import functools

import jax
import jax.numpy as jnp
from jax import lax
from jax.experimental import pallas as pl
from jax.experimental.pallas import tpu as pltpu
from jax.sharding import PartitionSpec as P

AXES = ("tm", "cam", "head")
HD = 128
WMAX = 4
PAIR = 2
TILE = 256
LOG2E = 1.4426950408889634
MIB = 1 << 20
ANY = pl.BlockSpec(memory_space=pl.ANY)
VMEM = pl.BlockSpec(memory_space=pltpu.VMEM)
SMEM = pl.BlockSpec(memory_space=pltpu.SMEM)
PARAMS = pltpu.CompilerParams(vmem_limit_bytes=64 * MIB)
SMALL = pl.CostEstimate(flops=10**9, bytes_accessed=1000, transcendentals=0)


def pairs_of(sizes, move):
    tm, cam, head = sizes
    flat = lambda t, c, h: (t * cam + c) * head + h
    return [
        (flat(t, c, h), flat(*move(t, c, h)))
        for t in range(tm)
        for c in range(cam)
        for h in range(head)
    ]


def x_low():
    return lax.axis_index("tm") % 2


def bf16(*shape):
    return jax.ShapeDtypeStruct(shape, jnp.bfloat16)


def project_kernel(blocks, chunks, tokens, w3, *refs):
    outs, (flat, w, sem_t, sem_w) = refs[:-4], refs[-4:]
    mine = x_low()
    depth = flat.shape[1] // chunks
    steps = []
    for k in range(chunks):
        ks = pl.ds(k * depth, depth)
        copies = [pltpu.make_async_copy(tokens.at[:, ks], flat.at[:, ks], sem_t.at[k])]
        for i, (which, own, _, _) in enumerate(blocks):
            col = pl.multiple_of(PAIR * HD * (mine if own else 1 - mine), PAIR * HD)
            copies.append(
                pltpu.make_async_copy(
                    w3.at[which, ks, pl.ds(col, PAIR * HD)],
                    w.at[ks, pl.ds(i * PAIR * HD, PAIR * HD)],
                    sem_w.at[k, i],
                )
            )
        steps.append(copies)
        for copy in copies:
            copy.start()
    total = None
    for k, copies in enumerate(steps):
        for copy in copies:
            copy.wait()
        ks = slice(k * depth, (k + 1) * depth)
        made = jnp.dot(flat[:, ks], w[ks, :], preferred_element_type=jnp.float32)
        total = made if total is None else total + made
    total = total.astype(jnp.bfloat16)
    for i, (_, _, out, at) in enumerate(blocks):
        for head in range(PAIR):
            col = (i * PAIR + head) * HD
            piece = total[:, col : col + HD].reshape(-1, TILE, HD)
            if at:
                outs[out + head][(0,) + at] = piece
            else:
                outs[out][head] = piece


def project(blocks, shapes, tokens, w3):
    rows, width = tokens.shape
    chunks = 4
    return pl.pallas_call(
        functools.partial(project_kernel, blocks, chunks),
        out_shape=shapes,
        in_specs=[ANY, ANY],
        out_specs=[VMEM] * len(shapes),
        scratch_shapes=[
            pltpu.VMEM((rows, width), jnp.bfloat16),
            pltpu.VMEM((width, len(blocks) * PAIR * HD), jnp.bfloat16),
            pltpu.SemaphoreType.DMA((chunks,)),
            pltpu.SemaphoreType.DMA((chunks, len(blocks))),
        ],
        compiler_params=PARAMS,
        cost_estimate=SMALL,
    )(tokens, w3)


def run_copies(pairs, sems):
    copies = [pltpu.make_async_copy(src, dst, sems.at[i]) for i, (src, dst) in enumerate(pairs)]
    for copy in copies:
        copy.start()
    for copy in copies:
        copy.wait()


def gather_kernel(kvx, kvm, four, halo, sems):
    mine = x_low()
    pairs = [(kvm, four.at[:, pl.ds(2 * mine, 2)]), (kvx, four.at[:, pl.ds(2 - 2 * mine, 2)])]

    @pl.when(mine == 0)
    def _():
        run_copies(pairs + [(kvm.at[:, 1], halo.at[:, 0]), (kvx, halo.at[:, pl.ds(1, 2)])], sems)

    @pl.when(mine == 1)
    def _():
        run_copies(pairs + [(kvx.at[:, 1], halo.at[:, 0]), (kvm, halo.at[:, pl.ds(1, 2)])], sems)


def gather(kvx, kvm):
    return pl.pallas_call(
        gather_kernel,
        out_shape=[bf16(2, 4, TILE, HD), bf16(2, 3, TILE, HD)],
        in_specs=[ANY] * 2,
        out_specs=[VMEM] * 2,
        scratch_shapes=[pltpu.SemaphoreType.DMA((4,))],
        compiler_params=PARAMS,
        cost_estimate=SMALL,
    )(kvx, kvm)


def attend_pairs(plan, count, off, bias, q, keys, values, peak, acc, bufs, at_step=None):
    score_a, score_b, weight_a, weight_b = bufs
    scale = LOG2E / HD**0.5

    def scored(i, scores):
        scores[...] = lax.dot_general(
            q[plan[0, i]], keys[plan[1, i]], (((1,), (1,)), ((), ())), preferred_element_type=jnp.float32
        )

    def weighed(i, scores, weights):
        at = plan[0, i]
        here = scores[...] * scale + (bias + off[i])
        old = peak[at]
        new = jnp.maximum(old, jnp.max(here, axis=1, keepdims=True))
        weights[...] = jnp.exp2(here - new[:, :1]).astype(jnp.bfloat16)
        shrink = jnp.exp2(old - new)
        peak[at] = new
        acc[at] = acc[at] * jnp.concatenate([shrink, shrink], axis=1)

    def added(i, weights):
        at = plan[0, i]
        acc[at] = acc[at] + jnp.dot(weights[...], values[plan[1, i]], preferred_element_type=jnp.float32)

    scored(0, score_a)
    weighed(0, score_a, weight_a)
    scored(1, score_b)

    def step(j, carry):
        if at_step is not None:
            at_step(j)
        i = 2 * j
        scored(i + 2, score_a)
        weighed(i + 1, score_b, weight_b)
        added(i, weight_a)
        scored(i + 3, score_b)
        weighed(i + 2, score_a, weight_a)
        added(i + 1, weight_b)
        return carry

    lax.fori_loop(0, lax.div(count + 1, 2), step, 0)


def plan_pairs(window, plan, off):
    count = 4 * window
    for back in range(WMAX):
        for frame in range(4):
            here = 4 * back + frame
            plan[0, here] = frame
            plan[1, here] = 3 + frame - back
            off[here] = 0.0
    for more in range(3):
        plan[0, count + more] = 0
        plan[1, count + more] = 3
        off[count + more] = -jnp.inf
    return count


def edge_bias(edges):
    cam, count = lax.axis_index("cam"), lax.axis_size("cam")
    left, right = edges[(cam + count - 1) % count], edges[cam]
    spot = lax.broadcasted_iota(jnp.int32, (1, 3 * TILE), 1)
    seen = (spot >= TILE - left * (TILE // 8)) & (spot < 2 * TILE + right * (TILE // 8))
    return jnp.where(seen, 0.0, -jnp.inf).astype(jnp.float32)


def started(pairs, sems):
    copies = [pltpu.make_async_copy(src, dst, sem) for (src, dst), sem in zip(pairs, sems)]
    for copy in copies:
        copy.start()
    return copies


PLACES = (1, 0, 2)


def attend_kernel(head, windows, edges, q_own, q_far, *refs):
    pieces, (out_own, out_far, q, keys, values, peak, acc, *bufs, plan, off, sems) = refs[:6], refs[6:]
    mine = x_low()
    pairs = [(q_own.at[head], q.at[pl.ds(2 * mine, 2)]), (q_far.at[head], q.at[pl.ds(2 - 2 * mine, 2)])]
    for n, (piece, frames) in enumerate(zip(pieces, [pl.ds(3, 4)] * 3 + [pl.ds(0, 3)] * 3)):
        rows = pl.ds(PLACES[n % 3] * TILE, TILE)
        pairs.append((piece.at[0], keys.at[frames, rows]))
        pairs.append((piece.at[1], values.at[frames, rows, pl.ds(0, HD)]))
    copies = started(pairs[:8], [sems.at[i] for i in range(8)])
    values[:, :, HD:] = jnp.ones((values.shape[0], 3 * TILE, HD), jnp.bfloat16)
    acc[...] = jnp.zeros_like(acc)
    peak[...] = jnp.full_like(peak, -jnp.inf)
    count = plan_pairs(windows[PAIR * mine + head], plan, off)
    for copy in copies:
        copy.wait()
    copies = started(pairs[8:], [sems.at[i] for i in range(8, len(pairs))])

    def earlier(j):
        @pl.when(j == 1)
        def _():
            for copy in copies:
                copy.wait()

    attend_pairs(plan, count, off, edge_bias(edges), q, keys, values, peak, acc, bufs, earlier)
    for out, first in ((out_own, 2 * mine), (out_far, 2 - 2 * mine)):
        for n in range(2):
            done = acc[first + n]
            out[n] = (done[:, :HD] / done[:, HD:]).astype(jnp.bfloat16)


def attend(head, windows, edges, q_own, q_far, pieces):
    return pl.pallas_call(
        functools.partial(attend_kernel, head),
        out_shape=[bf16(2, TILE, HD)] * 2,
        in_specs=[SMEM, SMEM] + [ANY] * (2 + len(pieces)),
        out_specs=[VMEM] * 2,
        scratch_shapes=[
            pltpu.VMEM((4, TILE, HD), jnp.bfloat16),
            pltpu.VMEM((7, 3 * TILE, HD), jnp.bfloat16),
            pltpu.VMEM((7, 3 * TILE, 2 * HD), jnp.bfloat16),
            pltpu.VMEM((4, TILE, HD), jnp.float32),
            pltpu.VMEM((4, TILE, 2 * HD), jnp.float32),
            pltpu.VMEM((TILE, 3 * TILE), jnp.float32),
            pltpu.VMEM((TILE, 3 * TILE), jnp.float32),
            pltpu.VMEM((TILE, 3 * TILE), jnp.bfloat16),
            pltpu.VMEM((TILE, 3 * TILE), jnp.bfloat16),
            pltpu.SMEM((2, 4 * WMAX + 4), jnp.int32),
            pltpu.SMEM((4 * WMAX + 4,), jnp.float32),
            pltpu.SemaphoreType.DMA((14,)),
        ],
        compiler_params=PARAMS,
        cost_estimate=SMALL,
    )(windows, edges, q_own, q_far, *pieces)


def mix_kernel(*refs):
    pieces, (w_out, w_mine, w_core, out, first, second, w, made, sem_a, sem_w, sem_o) = refs[:8], refs[8:]
    mine, core, head = x_low(), lax.axis_index("cam") % 2, lax.axis_index("head")
    part = PAIR * HD
    width = w.shape[1]
    steps = made.shape[0]
    half = width // steps
    rows = lambda at: pl.ds(pl.multiple_of(at, part), part)
    pairs = []
    for n, piece in enumerate(pieces):
        kind = n % 4
        held = (first, second)[kind // 2]
        pairs.append((piece, held.at[:, :, pl.ds((kind % 2 * PAIR + n // 4) * HD, HD)]))
    inputs = started(pairs, [sem_a.at[i] for i in range(8)])
    weights = []
    for n in range(steps):
        cols = pl.ds(n * half, half)
        there = pl.ds(pl.multiple_of(head * width + n * half, half), half)
        pairs = [
            (w_out.at[rows(part * mine), there], w.at[pl.ds(0, part), cols]),
            (w_out.at[rows(part * (1 - mine)), there], w.at[pl.ds(part, part), cols]),
            (w_mine.at[:, cols], w.at[rows(jnp.where(core == mine, 2, 3) * part), cols]),
            (w_core.at[:, cols], w.at[rows(jnp.where(core == mine, 3, 2) * part), cols]),
        ]
        weights.append(started(pairs, [sem_w.at[n, i] for i in range(4)]))
    for copy in inputs:
        copy.wait()

    def group(held, at, cols):
        total = jnp.dot(
            held[...].reshape(2 * TILE, 2 * part), w[at : at + 2 * part, cols], preferred_element_type=jnp.float32
        )
        return total.astype(jnp.bfloat16).astype(jnp.float32)

    outs = []
    for n in range(steps):
        for copy in weights[n]:
            copy.wait()
        cols = slice(n * half, (n + 1) * half)
        made[n] = (group(first, 0, cols) + group(second, 2 * part, cols)).astype(jnp.bfloat16)
        outs += started([(made.at[n], out.at[:, pl.ds(n * half, half)])], [sem_o.at[n]])
    for copy in outs:
        copy.wait()


def mix(attended, w_out, w_mine, w_core):
    rows = 2 * TILE
    width = w_out.shape[1] // 2
    return pl.pallas_call(
        mix_kernel,
        out_shape=bf16(rows, width),
        in_specs=[ANY] * 11,
        out_specs=ANY,
        scratch_shapes=[
            pltpu.VMEM((2, TILE, 2 * PAIR * HD), jnp.bfloat16),
            pltpu.VMEM((2, TILE, 2 * PAIR * HD), jnp.bfloat16),
            pltpu.VMEM((4 * PAIR * HD, width), jnp.bfloat16),
            pltpu.VMEM((4, rows, width // 4), jnp.bfloat16),
            pltpu.SemaphoreType.DMA((8,)),
            pltpu.SemaphoreType.DMA((4, 4)),
            pltpu.SemaphoreType.DMA((4,)),
        ],
        compiler_params=PARAMS,
        cost_estimate=SMALL,
    )(*attended, w_out, w_mine, w_core)


def body(tokens, w_qkv, w_out, window_len, edge_counts, context_kv):
    frames, cols, row_count, width = tokens.shape
    sizes = tuple(lax.axis_size(axis) for axis in AXES)
    tm_count, cam_count, _ = sizes
    tm, cam, x_hi = (lax.axis_index(axis) for axis in AXES)
    x_lo, core = tm % 2, cam % 2

    def moved(move):
        pairs = pairs_of(sizes, move)
        return lambda shard: lax.ppermute(shard, AXES, pairs)

    to_mate = moved(lambda t, c, h: (t ^ 1, c, h))
    to_over = moved(lambda t, c, h: (t, c, 1 - h))
    to_diag = moved(lambda t, c, h: (t ^ 1, c, 1 - h))
    to_later = moved(lambda t, c, h: ((t + 2) % tm_count, c, h))
    to_right = moved(lambda t, c, h: (t, (c + 1) % cam_count, h))
    to_left = moved(lambda t, c, h: (t, (c - 1) % cam_count, h))
    to_core = moved(lambda t, c, h: (t, c ^ 1, h))
    wide = lambda shard: [shard, to_right(shard), to_left(shard)]

    flat = tokens.reshape(frames * cols * row_count, width)
    w3 = jnp.transpose(w_qkv, (1, 0, 2))
    kv_shape = bf16(1, 2, frames, TILE, HD)
    q_shape = bf16(PAIR, frames, TILE, HD)

    sent = project([(1, False, 0, (0,)), (2, False, 0, (1,))], [kv_shape] * 2, flat, w3)
    hold = lambda x, *after: lax.optimization_barrier((x, after))[0]
    kvx = [to_mate(sent[0][0])]
    *kvm, q_sent, q_own = project(
        [(1, True, 0, (0,)), (2, True, 0, (1,)), (0, False, 2, ()), (0, True, 3, ())],
        [kv_shape] * 2 + [q_shape] * 2,
        hold(flat, sent),
        w3,
    )
    kvx.append(to_mate(hold(sent[1], q_own)[0]))
    q_far = to_mate(hold(q_sent, kvx[0]))

    four, later = [], []
    for head in range(PAIR):
        one, halo = gather(kvx[head], kvm[head][0])
        later.append(to_later(halo))
        outer = hold(one, four[0]) if head else one
        four.append([one, to_right(outer), to_left(outer)])
    halo = []
    for head in range(PAIR):
        ctx = lax.dynamic_slice_in_dim(hold(context_kv, four[1][0]), (PAIR * x_lo + head) * HD, HD, 4)
        ctx = jnp.transpose(ctx.reshape(WMAX - 1, TILE, 2, HD), (2, 0, 1, 3))
        halo.append(wide(jnp.where(tm < 2, ctx, hold(later[head], ctx))))

    half = w_out.shape[1] // 2
    w_part = lax.dynamic_slice(
        hold(w_out, four[0]), (core * PAIR * HD, (1 - x_hi) * half), (PAIR * HD, half)
    )
    w_mine = to_diag(w_part)

    pieces = []
    for head in range(PAIR):
        mine, mates = attend(head, window_len, edge_counts, q_own, q_far, four[head] + halo[head])
        if head == 0:
            w_core = to_core(hold(w_mine, mine))
        else:
            mine, mates, pieces = lax.optimization_barrier((mine, mates, pieces))
        pieces.append([mine, to_mate(mates), to_over(mine), to_diag(mates)])
    out = mix(pieces[0] + pieces[1], w_out, w_mine, w_core)
    return out.reshape(frames, cols, row_count, -1)


def solution(mesh):
    placed = (
        P("tm", "cam", None, None),
        P(None, None, "head"),
        P("head", None),
        P("head"),
        P(),
        P(None, "cam", None, None, "head"),
    )
    return jax.shard_map(
        body, mesh=mesh, in_specs=placed, out_specs=P("tm", "cam", None, "head"), check_vma=False
    )
```
